32 devices in a mesh: groups: 2 (over y), cg: 16 (over z, x, core).
Axes of the slice: x: 2, y: 2, z: 4, core: 2. Of those that a mesh axis runs over, the one named last changes fastest.
Arguments:
- embeddings: bfloat16 [8192, 1024], P(('groups', 'cg')), parts along dimension 0, may hold values from -2000 to 2000
- destination: int32 [8192, 1], P(('groups', 'cg')), parts along dimension 0, may hold values from 0 to 15; in each aligned block of 256 rows (0 to 255, 256 to 511, ...) at most 32 rows name the same one
- valid_row: int32 [8192], P(('groups', 'cg')), parts along dimension 0, may hold values 0 or 1
Outputs:
- closest: float32 [8192], P(('groups', 'cg')), parts along dimension 0
The draws below stay inside these ranges and needn't reach their ends.
There are 2 independent parts, one for each index of `groups`. The reference program is written for one: setup_inputs(seed, part) draws one part's arguments, and reference() takes and returns one part's arrays. A program takes and returns all parts, laid end to end along the dimension named above; each array names one. Nothing has to cross between parts.
Inputs may be any that keep to these rules, and one draw needn't show every extreme that they name: Among the documents of one device no destination appears more than 32 times, and some destination appears exactly 32 times on some device.
All inputs are finite; a program needn't handle non-finite values. No bound on the sum of `valid_row` on one device may be relied on, other than what follows from the above.
Results may differ from the reference program's by a relative error of at most 0.0005.
Values may be sent and summed in bfloat16 or wider, within the bound.
A program may use at most 64 MiB of HBM per device.

```python
import math
import jax
import jax.numpy as jnp
import numpy as np
from jax import lax

D = 1024
ROWS_DEV = 256
TEAM = 4
CAP = 32
TOKENS = 4096
N_CG = 16


def draw_embeddings(key, part):
    key = jax.random.fold_in(key, 5)
    subkeys = jax.random.split(key, 7)
    labels = jax.random.randint(subkeys[6], (TOKENS,), 0, 64)
    centers = jnp.clip(jax.random.normal(subkeys[0], (64, D), jnp.float32), -6.0, 6.0)
    weight = jax.random.uniform(subkeys[1], (TOKENS, 1), jnp.float32, 0.0, 1.5)
    columns = jnp.exp(jax.random.uniform(subkeys[2], (1, D), jnp.float32, 0.0, math.log(10.0)))
    row_scale = jnp.exp(jax.random.uniform(subkeys[3], (TOKENS, 1), jnp.float32, 0.0, math.log(10.0)))
    noise = jnp.clip(jax.random.normal(subkeys[4], (TOKENS, D), jnp.float32), -6.0, 6.0)
    mixture = noise + weight * centers[labels]
    return (mixture * columns * row_scale).astype(jnp.bfloat16)


def place_ends(values, own_key, low, top_value):
    place = [jax.random.randint(jax.random.fold_in(own_key, axis), (), 0, length) for axis, length in enumerate(values.shape)]
    main_axis = values.shape.index(max(values.shape))
    next_to = place[:main_axis] + [(place[main_axis] + 1) % values.shape[main_axis]] + place[main_axis + 1:]
    return values.at[tuple(place)].set(low).at[tuple(next_to)].set(top_value)


def deal_out(key, own, number, rows, amount, top, bound, lean):
    sequence = jax.random.permutation(key, amount)
    heavy_load, ordinary = portions_of(amount, rows * top, bound, lean, True), portions_of(amount, rows * top, bound, lean, False)
    places = jnp.arange(amount)

    def named(lengths, turn):
        used = int((lengths > 0).sum())
        fixed = max(1, used // 4)
        shifted = fixed + (places - fixed + turn * (used - fixed)) % max(1, amount - fixed)
        return jnp.zeros((amount,), jnp.int32).at[sequence[jnp.where(places < fixed, places, shifted)]].set(jnp.asarray(lengths, jnp.int32))

    lengths = jnp.where(number % 4 == 0, named(heavy_load, number // 4), named(ordinary, number - number // 4 - 1))
    mixed = jax.random.permutation(jax.random.fold_in(own, 3), amount)
    giver, receiver = mixed[0:amount // 2 * 2:2], mixed[1:amount // 2 * 2:2]
    room = jnp.minimum(lengths[giver] - 1, bound - lengths[receiver]) // 2
    room = jnp.where((giver == sequence[0]) | (receiver == sequence[0]) | (lengths[receiver] == 0), 0, jnp.maximum(room, 0))
    shifted = jax.random.randint(jax.random.fold_in(own, 4), (amount // 2,), 0, 1 << 20) % (room + 1)
    lengths = lengths.at[giver].add(-shifted).at[receiver].add(shifted)
    items = jnp.searchsorted(jnp.cumsum(lengths), jnp.arange(rows * top), side="right").astype(jnp.int32)
    table = items.reshape(top, rows).T
    table = table[jax.random.permutation(jax.random.fold_in(own, 1), rows)]
    turn = jax.random.randint(jax.random.fold_in(own, 2), (rows, 1), 0, top)
    return jnp.take_along_axis(table, (jnp.arange(top)[None, :] + turn) % top, axis=1)


def portions_of(count, total, reach, slope, full):
    weights = [(1 << 20) // math.isqrt(grade ** slope) + 1 for grade in range(1, count + 1)]
    largest = reach if full else min(reach, max(-(-total // count), total * weights[0] // sum(weights)))
    least = 1 if total - largest >= count - 1 else 0
    given, rest = [largest] + [least] * (count - 1), total - largest - least * (count - 1)
    while rest > 0:
        free = [i for i in range(1, count) if given[i] < largest] or [i for i in range(1, count) if given[i] < reach]
        mass, remaining = sum([weights[i] for i in free]), rest
        for i in free:
            more = min(reach - given[i], max(1, remaining * weights[i] // mass), rest)
            given[i] = given[i] + more
            rest = rest - more
    return np.array(given)


def setup_inputs(seed: int = 0, part: int = 0) -> dict:
    key_of = jax.random.split(jax.random.key(seed), 4)
    own_keys = jax.random.split(jax.random.fold_in(key_of[3], part), 4)
    embeddings = draw_embeddings(jax.random.fold_in(jax.random.fold_in(key_of[3], part), 71), part)
    destination_keys = jax.random.split(jax.random.fold_in(own_keys[1], 1), TOKENS // ROWS_DEV)
    destination_turns = jax.random.permutation(jax.random.fold_in(own_keys[1], 3), TOKENS // ROWS_DEV)
    destination = jax.vmap(lambda own, number: deal_out(jax.random.fold_in(own_keys[1], 2), own, number, ROWS_DEV, N_CG, 1, CAP, 2))(destination_keys, destination_turns).reshape((TOKENS, 1))
    valid_row = place_ends((jax.random.randint(own_keys[2], (TOKENS,), 0, 8) < 7).astype(jnp.int32), jax.random.fold_in(own_keys[2], 1), 0, 1)
    return {"embeddings": embeddings, "destination": destination, "valid_row": valid_row}


epsilon = 1e-06

def normalize(embeddings):
    values = embeddings.astype(jnp.float32)
    inv_scale = lax.rsqrt(lax.optimization_barrier(jnp.mean(values * values, axis=1, keepdims=True)) + epsilon)
    return (values * inv_scale * values.shape[1] ** (-0.5)).astype(jnp.bfloat16)

def reference(embeddings, destination, valid_row):
    unit_rows = normalize(embeddings)
    team_of = destination[:, 0] // TEAM
    row_tag = jnp.where(valid_row == 1, 1, 0).astype(jnp.int32)
    pool_size = 2 * ROWS_DEV * TEAM
    pool_index = jnp.arange(pool_size, dtype=jnp.int32)

    def one_team(team_index):
        members = team_of == team_index
        member_count = jnp.sum(members.astype(jnp.int32))
        chosen = jnp.nonzero(members, size=pool_size, fill_value=0)[0].astype(jnp.int32)
        present = pool_index < member_count
        picked = unit_rows[chosen]
        picked_tag = jnp.where(present, row_tag[chosen], 0)
        similar = jnp.dot(picked, picked.T, preferred_element_type=jnp.float32)
        matches = (picked_tag[:, None] == picked_tag[None, :]) & (picked_tag[:, None] > 0) & (pool_index[:, None] != pool_index[None, :])
        closest = lax.optimization_barrier(jnp.max(jnp.where(matches, similar, -1.0), axis=1))
        return (jnp.where(present, chosen, TOKENS).astype(jnp.int32), closest)
    where_to, values = lax.map(one_team, jnp.arange(N_CG // TEAM, dtype=jnp.int32))
    result = jnp.full((TOKENS + 1,), -1.0, jnp.float32).at[where_to.reshape(-1)].set(values.reshape(-1))
    return result[:TOKENS]
```

```python
import jax
import jax.numpy as jnp
from jax import lax
from jax.experimental import pallas as pl
from jax.experimental.pallas import tpu as pltpu
from jax.sharding import PartitionSpec as P

TEAM = 4


epsilon = 1e-06


def from_partner(array, axis, stride):
    return lax.ppermute(array, axis, [(i, i ^ 1 << stride) for i in range(lax.axis_size(axis))])


def normalize(embeddings):
    values = embeddings.astype(jnp.float32)
    inv_scale = lax.rsqrt(jnp.mean(values * values, axis=1, keepdims=True) + epsilon)
    return (values * inv_scale * values.shape[1] ** (-0.5)).astype(jnp.bfloat16)


def closest_in(own_rows, own_tag, own_key, other_rows, other_tag, other_key):
    similar = jnp.einsum("id,jd->ij", own_rows, other_rows, preferred_element_type=jnp.float32)
    matches = (
        (own_tag[:, None] == other_tag[None, :])
        & (own_tag[:, None] > 0)
        & (own_key[:, None] != other_key[None, :])
    )
    return jnp.max(jnp.where(matches, similar, -1.0), axis=1)


def on_device(embeddings, destination, valid_row):
    groups = lax.axis_size("cg")
    row_count, feat_width = embeddings.shape
    capacity = 2 * row_count // groups
    slot_count = groups * capacity
    member = lax.axis_index("cg") % TEAM
    unit_rows = normalize(embeddings)
    target = destination[:, 0]
    row_tag = jnp.where(valid_row == 1, 1, 0).astype(jnp.int32)
    places = jnp.arange(groups, dtype=jnp.int32)
    onehot = (target[:, None] == places[None, :]).astype(jnp.float32)
    row_order = jnp.arange(row_count, dtype=jnp.int32)
    earlier = (row_order[:, None] > row_order[None, :]).astype(jnp.float32)
    before = jnp.dot(earlier, onehot, precision=lax.Precision.HIGHEST)
    row_rank = jnp.sum(before * onehot, axis=1).astype(jnp.int32)
    row_slot = target * capacity + row_rank
    outgoing = jnp.zeros((slot_count, feat_width), jnp.bfloat16).at[row_slot].set(unit_rows)
    out_tags = jnp.zeros((slot_count,), jnp.int32).at[row_slot].set(row_tag)
    team_tags = jnp.repeat(out_tags.reshape(groups // TEAM, TEAM * capacity), TEAM, axis=0)
    positions = jnp.arange(slot_count, dtype=jnp.int32)
    own_key = member * slot_count + positions
    arrived, pool_tags = (
        lax.all_to_all(
            outgoing.reshape(groups, capacity, feat_width),
            "cg",
            split_axis=0,
            concat_axis=0,
            tiled=True,
        ),
        lax.all_to_all(team_tags, "cg", split_axis=0, concat_axis=0, tiled=True),
    )
    own_rows = arrived.reshape(slot_count, feat_width)

    def tags_of(owner_member):
        return lax.dynamic_slice_in_dim(pool_tags, owner_member * capacity, capacity, 1).reshape(
            slot_count
        )

    own_tag = tags_of(member)
    closest = closest_in(own_rows, own_tag, own_key, own_rows, own_tag, own_key)
    first_rows = from_partner(own_rows, "cg", 0)
    first_member = member ^ 1
    closest = jnp.maximum(
        closest,
        closest_in(
            own_rows,
            own_tag,
            own_key,
            first_rows,
            tags_of(first_member),
            first_member * slot_count + positions,
        ),
    )
    for held_rows, offset in ((own_rows, 2), (first_rows, 3)):
        far_rows = from_partner(held_rows, "cg", 1)
        owner_member = member ^ offset
        closest = jnp.maximum(
            closest,
            closest_in(
                own_rows,
                own_tag,
                own_key,
                far_rows,
                tags_of(owner_member),
                owner_member * slot_count + positions,
            ),
        )
    answers = lax.all_to_all(
        closest.reshape(groups, capacity), "cg", split_axis=0, concat_axis=0, tiled=True
    )
    return answers.reshape(slot_count)[row_slot]


MESH = pl.DeviceIdType.MESH
PLANES = 4
CHUNKS = 4
TAG_ROWS = 16
A, B, C = 4, 5, 6


def pieces(row_count, feat_width):
    step = row_count // CHUNKS
    return [(row_count, TAG_ROWS, row_count)] + [(i * step, step, feat_width) for i in range(CHUNKS)]


def kernel(emb_ref, tag_ref, out_ref, held, cols, outbox, inbox, send_sem, recv_sem, back_send, back_recv):
    rows, width = emb_ref.shape
    parts = pieces(rows, width)
    group = lax.axis_index("groups")
    me = lax.axis_index("cg")
    z, p = me // TEAM, me % TEAM
    core_p = p + 1 - 2 * (p % 2)
    x_p = (p + 2) % TEAM
    diag_p = (core_p + 2) % TEAM

    def device(plane, place):
        return (group, plane * TEAM + place)

    barrier = pltpu.get_barrier_semaphore()
    for k in range(1, TEAM):
        pl.semaphore_signal(barrier, inc=1, device_id=device(z, (p + k) % TEAM), device_id_type=MESH)
    for k in range(1, PLANES):
        pl.semaphore_signal(barrier, inc=1, device_id=device((z + k) % PLANES, p), device_id_type=MESH)

    for i in range(4):
        block = pl.ds(i * (rows // 4), rows // 4)
        values = emb_ref[block, :].astype(jnp.float32)
        inv_scale = lax.rsqrt(jnp.mean(values * values, axis=1, keepdims=True) + epsilon)
        held[p, block, :] = (values * inv_scale * width ** (-0.5)).astype(jnp.bfloat16)
    held[p, pl.ds(rows, TAG_ROWS), pl.ds(0, rows)] = tag_ref[...]
    pl.semaphore_wait(barrier, TEAM - 1 + PLANES - 1)

    def piece(slot, k):
        start, size, lanes = parts[k]
        return held.at[slot, pl.ds(start, size), pl.ds(0, lanes)]

    def copy(k, source, target, flow, to):
        return pltpu.make_async_remote_copy(
            src_ref=piece(source, k),
            dst_ref=piece(target, k),
            send_sem=send_sem.at[flow, k],
            recv_sem=recv_sem.at[target, k],
            device_id=to,
            device_id_type=MESH,
        )

    up, down = (z + 1) % PLANES, (z + PLANES - 1) % PLANES
    second = jnp.where(z == 1, B, A)
    core_own = lambda k: copy(k, p, p, 0, device(z, core_p))
    x_own = lambda k: copy(k, p, p, 1, device(z, x_p))
    core_pass = lambda k: copy(k, x_p, x_p, 2, device(z, core_p))
    up_own = lambda k: copy(k, p, A, 3, device(up, p))
    up_first = lambda k: copy(k, A, second, 4, device(up, p))
    up_second = lambda k: copy(k, B, B, 5, device(up, p))
    down_own = lambda k: copy(k, p, C, 6, device(down, p))
    every = range(len(parts))

    def arrived(slot, k):
        copy(k, slot, slot, 0, device(z, core_p)).wait_recv()

    for k in every:
        pl.when(z <= 1)(lambda: up_own(k).start())
        pl.when(z == 3)(lambda: down_own(k).start())
        x_own(k).start()
    for k in every:
        core_own(k).start()

    def tag_lanes(slot):
        return held[slot, pl.ds(rows, TAG_ROWS), pl.ds(0, rows)].astype(jnp.float32)[0:1]

    def tag_down(slot):
        return jnp.broadcast_to(tag_lanes(slot), (128, rows)).T

    def compare(slot, own, first):
        tags = tag_down(slot)
        tags = jnp.concatenate([tags] * (rows // 128), axis=1)

        def step(q, best):
            similar = lax.dot_general(
                held[slot, pl.ds(0, rows), :],
                held[q, pl.ds(0, rows), :],
                (((1,), (1,)), ((), ())),
                preferred_element_type=jnp.float32,
            )
            other = tag_lanes(q)
            match = tags == jnp.where(other < 0, -2.0, other)
            if own:
                here = lax.broadcasted_iota(jnp.int32, (rows, rows), 0)
                there = lax.broadcasted_iota(jnp.int32, (rows, rows), 1)
                match = match & (here + jnp.where(q == p, 0, rows) != there)
            similar = jnp.where(match, similar, -1.0)
            if not own:
                top = jnp.broadcast_to(jnp.max(similar, axis=0, keepdims=True), (8, rows))
                cols[q] = top if first else jnp.maximum(cols[q], top)
            for i in range(rows // 128):
                best = jnp.maximum(best, similar[:, i * 128:(i + 1) * 128])
            return best

        best = lax.fori_loop(0, TEAM, step, jnp.full((rows, 128), -1.0, jnp.float32))
        return jnp.broadcast_to(jnp.max(best.T, axis=0, keepdims=True), (8, rows))

    def back(n, target, to):
        return pltpu.make_async_remote_copy(
            src_ref=outbox.at[n],
            dst_ref=inbox.at[target],
            send_sem=back_send.at[n],
            recv_sem=back_recv.at[target],
            device_id=to,
            device_id_type=MESH,
        )

    back_a = lambda: back(0, z, device(jnp.where(z == 1, 0, 1), p))
    back_b = lambda: back(1, z, device(0, p))
    back_c = lambda: back(2, z, device(3, p))
    back_q = lambda k: back(2 + k, PLANES + p, device(z, (p + k) % TEAM))

    def returned(target):
        back(0, target, device(z, core_p)).wait_recv()

    for k in every:
        @pl.when(z >= 1)
        def _():
            arrived(A, k)
            pl.when(z <= 2)(lambda: up_first(k).start())

        arrived(x_p, k)
        core_pass(k).start()
    for k in every:
        arrived(core_p, k)
    for k in every:
        arrived(diag_p, k)

    @pl.when(z >= 1)
    def _():
        outbox[0] = compare(A, False, True)
        back_a().start()

    closest = compare(p, True, False)

    @pl.when(z == 2)
    def _():
        for k in every:
            arrived(C, k)
        outbox[2] = compare(C, False, False)
        back_c().start()

    @pl.when(z >= 2)
    def _():
        for k in every:
            arrived(B, k)
            pl.when(z == 2)(lambda: up_second(k).start())
        outbox[1] = compare(B, False, False)
        back_b().start()

    @pl.when(z >= 1)
    def _():
        for k in range(1, TEAM):
            outbox[2 + k] = cols[(p + k) % TEAM]
            back_q(k).start()

    out_ref[...] = closest

    @pl.when(z >= 1)
    def _():
        best = cols[p]
        for k in range(1, TEAM):
            returned(PLANES + (p + k) % TEAM)
            best = jnp.maximum(best, inbox[PLANES + (p + k) % TEAM])
        out_ref[...] = jnp.maximum(out_ref[...], best)

    for source, readers in ((1, z == 0), (2, (z == 0) | (z == 1) | (z == 3)), (3, z <= 1)):
        @pl.when(readers)
        def _():
            returned(source)
            out_ref[...] = jnp.maximum(out_ref[...], inbox[source])

    for k in every:
        core_own(k).wait_send()
        x_own(k).wait_send()
        core_pass(k).wait_send()
        pl.when(z <= 1)(lambda: up_own(k).wait_send())
        pl.when((z == 1) | (z == 2))(lambda: up_first(k).wait_send())
        pl.when(z == 2)(lambda: up_second(k).wait_send())
        pl.when(z == 3)(lambda: down_own(k).wait_send())

    @pl.when(z >= 1)
    def _():
        back_a().wait_send()
        for k in range(1, TEAM):
            back_q(k).wait_send()

    pl.when(z >= 2)(lambda: back_b().wait_send())
    pl.when(z == 2)(lambda: back_c().wait_send())


def in_planes(embeddings, destination, valid_row):
    rows, width = embeddings.shape
    tag = jnp.where(valid_row == 1, destination[:, 0] // TEAM, -1).astype(jnp.bfloat16)
    count = len(pieces(rows, width))
    vmem = pl.BlockSpec(memory_space=pltpu.VMEM)
    closest = pl.pallas_call(
        kernel,
        out_shape=jax.ShapeDtypeStruct((8, rows), jnp.float32),
        in_specs=[vmem, vmem],
        out_specs=vmem,
        scratch_shapes=[
            pltpu.VMEM((TEAM + 3, rows + TAG_ROWS, width), jnp.bfloat16),
            pltpu.VMEM((TEAM, 8, rows), jnp.float32),
            pltpu.VMEM((6, 8, rows), jnp.float32),
            pltpu.VMEM((PLANES + TEAM, 8, rows), jnp.float32),
            pltpu.SemaphoreType.DMA((7, count)),
            pltpu.SemaphoreType.DMA((7, count)),
            pltpu.SemaphoreType.DMA((6,)),
            pltpu.SemaphoreType.DMA((PLANES + TEAM,)),
        ],
        compiler_params=pltpu.CompilerParams(
            collective_id=0, has_side_effects=True, vmem_limit_bytes=32 * 1024 * 1024
        ),
    )(embeddings, jnp.broadcast_to(tag[None, :], (TAG_ROWS, rows)))
    return closest[0]


def solution(mesh):
    return jax.shard_map(
        in_planes if mesh.shape["cg"] == PLANES * TEAM else on_device,
        mesh=mesh,
        in_specs=(P(("groups", "cg"), None), P(("groups", "cg"), None), P(("groups", "cg"))),
        out_specs=P(("groups", "cg")),
        check_vma=False,
    )
```

```python
import jax
import jax.numpy as jnp
from jax import lax
from jax.experimental import pallas as pl
from jax.experimental.pallas import tpu as pltpu
from jax.sharding import PartitionSpec as P

TEAM = 4


epsilon = 1e-06


def from_partner(array, axis, stride):
    return lax.ppermute(array, axis, [(i, i ^ 1 << stride) for i in range(lax.axis_size(axis))])


def normalize(embeddings):
    values = embeddings.astype(jnp.float32)
    inv_scale = lax.rsqrt(jnp.mean(values * values, axis=1, keepdims=True) + epsilon)
    return (values * inv_scale * values.shape[1] ** (-0.5)).astype(jnp.bfloat16)


def closest_in(own_rows, own_tag, own_key, other_rows, other_tag, other_key):
    similar = jnp.einsum("id,jd->ij", own_rows, other_rows, preferred_element_type=jnp.float32)
    matches = (
        (own_tag[:, None] == other_tag[None, :])
        & (own_tag[:, None] > 0)
        & (own_key[:, None] != other_key[None, :])
    )
    return jnp.max(jnp.where(matches, similar, -1.0), axis=1)


def on_device(embeddings, destination, valid_row):
    groups = lax.axis_size("cg")
    row_count, feat_width = embeddings.shape
    capacity = 2 * row_count // groups
    slot_count = groups * capacity
    member = lax.axis_index("cg") % TEAM
    unit_rows = normalize(embeddings)
    target = destination[:, 0]
    row_tag = jnp.where(valid_row == 1, 1, 0).astype(jnp.int32)
    places = jnp.arange(groups, dtype=jnp.int32)
    onehot = (target[:, None] == places[None, :]).astype(jnp.float32)
    row_order = jnp.arange(row_count, dtype=jnp.int32)
    earlier = (row_order[:, None] > row_order[None, :]).astype(jnp.float32)
    before = jnp.dot(earlier, onehot, precision=lax.Precision.HIGHEST)
    row_rank = jnp.sum(before * onehot, axis=1).astype(jnp.int32)
    row_slot = target * capacity + row_rank
    outgoing = jnp.zeros((slot_count, feat_width), jnp.bfloat16).at[row_slot].set(unit_rows)
    out_tags = jnp.zeros((slot_count,), jnp.int32).at[row_slot].set(row_tag)
    team_tags = jnp.repeat(out_tags.reshape(groups // TEAM, TEAM * capacity), TEAM, axis=0)
    positions = jnp.arange(slot_count, dtype=jnp.int32)
    own_key = member * slot_count + positions
    arrived, pool_tags = (
        lax.all_to_all(
            outgoing.reshape(groups, capacity, feat_width),
            "cg",
            split_axis=0,
            concat_axis=0,
            tiled=True,
        ),
        lax.all_to_all(team_tags, "cg", split_axis=0, concat_axis=0, tiled=True),
    )
    own_rows = arrived.reshape(slot_count, feat_width)

    def tags_of(owner_member):
        return lax.dynamic_slice_in_dim(pool_tags, owner_member * capacity, capacity, 1).reshape(
            slot_count
        )

    own_tag = tags_of(member)
    closest = closest_in(own_rows, own_tag, own_key, own_rows, own_tag, own_key)
    first_rows = from_partner(own_rows, "cg", 0)
    first_member = member ^ 1
    closest = jnp.maximum(
        closest,
        closest_in(
            own_rows,
            own_tag,
            own_key,
            first_rows,
            tags_of(first_member),
            first_member * slot_count + positions,
        ),
    )
    for held_rows, offset in ((own_rows, 2), (first_rows, 3)):
        far_rows = from_partner(held_rows, "cg", 1)
        owner_member = member ^ offset
        closest = jnp.maximum(
            closest,
            closest_in(
                own_rows,
                own_tag,
                own_key,
                far_rows,
                tags_of(owner_member),
                owner_member * slot_count + positions,
            ),
        )
    answers = lax.all_to_all(
        closest.reshape(groups, capacity), "cg", split_axis=0, concat_axis=0, tiled=True
    )
    return answers.reshape(slot_count)[row_slot]


MESH = pl.DeviceIdType.MESH
PLANES = 4
CHUNKS = 4
TAG_ROWS = 16
A, B, C = 4, 5, 6


def pieces(row_count, feat_width):
    step = row_count // CHUNKS
    return [(row_count, TAG_ROWS, row_count)] + [(i * step, step, feat_width) for i in range(CHUNKS)]


def kernel(emb_ref, tag_ref, out_ref, held, cols, outbox, inbox, send_sem, recv_sem, back_send, back_recv):
    rows, width = emb_ref.shape
    parts = pieces(rows, width)
    group = lax.axis_index("groups")
    me = lax.axis_index("cg")
    z, p = me // TEAM, me % TEAM
    core_p = p + 1 - 2 * (p % 2)
    x_p = (p + 2) % TEAM
    diag_p = (core_p + 2) % TEAM

    def device(plane, place):
        return (group, plane * TEAM + place)

    barrier = pltpu.get_barrier_semaphore()
    for k in range(1, TEAM):
        pl.semaphore_signal(barrier, inc=1, device_id=device(z, (p + k) % TEAM), device_id_type=MESH)
    for k in range(1, PLANES):
        pl.semaphore_signal(barrier, inc=1, device_id=device((z + k) % PLANES, p), device_id_type=MESH)

    for i in range(4):
        block = pl.ds(i * (rows // 4), rows // 4)
        values = emb_ref[block, :].astype(jnp.float32)
        inv_scale = lax.rsqrt(jnp.mean(values * values, axis=1, keepdims=True) + epsilon)
        held[p, block, :] = (values * inv_scale * width ** (-0.5)).astype(jnp.bfloat16)
    held[p, pl.ds(rows, TAG_ROWS), pl.ds(0, rows)] = tag_ref[...]
    pl.semaphore_wait(barrier, TEAM - 1 + PLANES - 1)

    def piece(slot, k):
        start, size, lanes = parts[k]
        return held.at[slot, pl.ds(start, size), pl.ds(0, lanes)]

    def copy(k, source, target, flow, to):
        return pltpu.make_async_remote_copy(
            src_ref=piece(source, k),
            dst_ref=piece(target, k),
            send_sem=send_sem.at[flow, k],
            recv_sem=recv_sem.at[target, k],
            device_id=to,
            device_id_type=MESH,
        )

    up, down = (z + 1) % PLANES, (z + PLANES - 1) % PLANES
    second = jnp.where(z == 1, B, A)
    core_own = lambda k: copy(k, p, p, 0, device(z, core_p))
    x_own = lambda k: copy(k, p, p, 1, device(z, x_p))
    core_pass = lambda k: copy(k, x_p, x_p, 2, device(z, core_p))
    up_own = lambda k: copy(k, p, A, 3, device(up, p))
    up_first = lambda k: copy(k, A, second, 4, device(up, p))
    up_second = lambda k: copy(k, B, B, 5, device(up, p))
    down_own = lambda k: copy(k, p, C, 6, device(down, p))
    every = range(len(parts))

    def arrived(slot, k):
        copy(k, slot, slot, 0, device(z, core_p)).wait_recv()

    for k in every:
        pl.when(z <= 1)(lambda: up_own(k).start())
        pl.when(z == 3)(lambda: down_own(k).start())
        x_own(k).start()
    for k in every:
        core_own(k).start()

    def tag_lanes(slot):
        return held[slot, pl.ds(rows, TAG_ROWS), pl.ds(0, rows)].astype(jnp.float32)[0:1]

    def compare(slot, own, first, start=0, size=rows):
        tags = jnp.broadcast_to(tag_lanes(slot)[:, start:start + size], (128, size)).T
        tags = jnp.concatenate([tags] * (rows // 128), axis=1)

        def step(q, best):
            similar = lax.dot_general(
                held[slot, pl.ds(start, size), :],
                held[q, pl.ds(0, rows), :],
                (((1,), (1,)), ((), ())),
                preferred_element_type=jnp.float32,
            )
            other = tag_lanes(q)
            match = tags == jnp.where(other < 0, -2.0, other)
            if own:
                here = lax.broadcasted_iota(jnp.int32, (size, rows), 0)
                there = lax.broadcasted_iota(jnp.int32, (size, rows), 1)
                match = match & (here + jnp.where(q == p, 0, rows) != there)
            similar = jnp.where(match, similar, -1.0)
            if not own:
                top = jnp.broadcast_to(jnp.max(similar, axis=0, keepdims=True), (8, rows))
                cols[q] = top if first else jnp.maximum(cols[q], top)
            for i in range(rows // 128):
                best = jnp.maximum(best, similar[:, i * 128:(i + 1) * 128])
            return best

        best = lax.fori_loop(0, TEAM, step, jnp.full((size, 128), -1.0, jnp.float32))
        return jnp.broadcast_to(jnp.max(best.T, axis=0, keepdims=True), (8, size))

    def back(n, target, to):
        return pltpu.make_async_remote_copy(
            src_ref=outbox.at[n],
            dst_ref=inbox.at[target],
            send_sem=back_send.at[n],
            recv_sem=back_recv.at[target],
            device_id=to,
            device_id_type=MESH,
        )

    back_a = lambda: back(0, z, device(jnp.where(z == 1, 0, 1), p))
    back_b = lambda: back(1, z, device(0, p))
    back_c = lambda: back(2, z, device(3, p))
    back_q = lambda k: back(2 + k, PLANES + p, device(z, (p + k) % TEAM))

    def returned(target):
        back(0, target, device(z, core_p)).wait_recv()

    for k in every:
        @pl.when(z >= 1)
        def _():
            arrived(A, k)
            pl.when(z <= 2)(lambda: up_first(k).start())

        arrived(x_p, k)
        core_pass(k).start()
    for k in every:
        arrived(core_p, k)
    for k in every:
        arrived(diag_p, k)

    @pl.when(z >= 1)
    def _():
        outbox[0] = compare(A, False, True)
        back_a().start()

    def pump(k):
        @pl.when(z >= 2)
        def _():
            arrived(B, k)
            pl.when(z == 2)(lambda: up_second(k).start())

    pump(0)
    pump(1)
    out_ref[...] = compare(p, True, False)
    pump(2)

    @pl.when(z == 2)
    def _():
        for k in every:
            arrived(C, k)
        outbox[2] = compare(C, False, False)
        back_c().start()

    half = rows // 2

    @pl.when(z >= 2)
    def _():
        outbox[1, :, pl.ds(0, half)] = compare(B, False, False, 0, half)

    pump(3)
    pump(4)

    @pl.when(z >= 2)
    def _():
        outbox[1, :, pl.ds(half, half)] = compare(B, False, False, half, half)
        back_b().start()

    @pl.when(z >= 1)
    def _():
        for k in range(1, TEAM):
            outbox[2 + k] = cols[(p + k) % TEAM]
            back_q(k).start()

    @pl.when(z >= 1)
    def _():
        best = cols[p]
        for k in range(1, TEAM):
            returned(PLANES + (p + k) % TEAM)
            best = jnp.maximum(best, inbox[PLANES + (p + k) % TEAM])
        out_ref[...] = jnp.maximum(out_ref[...], best)

    for source, readers in ((1, z == 0), (2, (z == 0) | (z == 1) | (z == 3)), (3, z <= 1)):
        @pl.when(readers)
        def _():
            returned(source)
            out_ref[...] = jnp.maximum(out_ref[...], inbox[source])

    for k in every:
        core_own(k).wait_send()
        x_own(k).wait_send()
        core_pass(k).wait_send()
        pl.when(z <= 1)(lambda: up_own(k).wait_send())
        pl.when((z == 1) | (z == 2))(lambda: up_first(k).wait_send())
        pl.when(z == 2)(lambda: up_second(k).wait_send())
        pl.when(z == 3)(lambda: down_own(k).wait_send())

    @pl.when(z >= 1)
    def _():
        back_a().wait_send()
        for k in range(1, TEAM):
            back_q(k).wait_send()

    pl.when(z >= 2)(lambda: back_b().wait_send())
    pl.when(z == 2)(lambda: back_c().wait_send())


def in_planes(embeddings, destination, valid_row):
    rows, width = embeddings.shape
    tag = jnp.where(valid_row == 1, destination[:, 0] // TEAM, -1).astype(jnp.bfloat16)
    count = len(pieces(rows, width))
    vmem = pl.BlockSpec(memory_space=pltpu.VMEM)
    closest = pl.pallas_call(
        kernel,
        out_shape=jax.ShapeDtypeStruct((8, rows), jnp.float32),
        in_specs=[vmem, vmem],
        out_specs=vmem,
        scratch_shapes=[
            pltpu.VMEM((TEAM + 3, rows + TAG_ROWS, width), jnp.bfloat16),
            pltpu.VMEM((TEAM, 8, rows), jnp.float32),
            pltpu.VMEM((6, 8, rows), jnp.float32),
            pltpu.VMEM((PLANES + TEAM, 8, rows), jnp.float32),
            pltpu.SemaphoreType.DMA((7, count)),
            pltpu.SemaphoreType.DMA((7, count)),
            pltpu.SemaphoreType.DMA((6,)),
            pltpu.SemaphoreType.DMA((PLANES + TEAM,)),
        ],
        compiler_params=pltpu.CompilerParams(
            collective_id=0, has_side_effects=True, vmem_limit_bytes=32 * 1024 * 1024
        ),
    )(embeddings, jnp.broadcast_to(tag[None, :], (TAG_ROWS, rows)))
    return closest[0]


def solution(mesh):
    return jax.shard_map(
        in_planes if mesh.shape["cg"] == PLANES * TEAM else on_device,
        mesh=mesh,
        in_specs=(P(("groups", "cg"), None), P(("groups", "cg"), None), P(("groups", "cg"))),
        out_specs=P(("groups", "cg")),
        check_vma=False,
    )
```

```python
import jax
import jax.numpy as jnp
from jax import lax
from jax.experimental import pallas as pl
from jax.experimental.pallas import tpu as pltpu
from jax.sharding import PartitionSpec as P

TEAM = 4


epsilon = 1e-06


def from_partner(array, axis, stride):
    return lax.ppermute(array, axis, [(i, i ^ 1 << stride) for i in range(lax.axis_size(axis))])


def normalize(embeddings):
    values = embeddings.astype(jnp.float32)
    inv_scale = lax.rsqrt(jnp.mean(values * values, axis=1, keepdims=True) + epsilon)
    return (values * inv_scale * values.shape[1] ** (-0.5)).astype(jnp.bfloat16)


def closest_in(own_rows, own_tag, own_key, other_rows, other_tag, other_key):
    similar = jnp.einsum("id,jd->ij", own_rows, other_rows, preferred_element_type=jnp.float32)
    matches = (
        (own_tag[:, None] == other_tag[None, :])
        & (own_tag[:, None] > 0)
        & (own_key[:, None] != other_key[None, :])
    )
    return jnp.max(jnp.where(matches, similar, -1.0), axis=1)


def on_device(embeddings, destination, valid_row):
    groups = lax.axis_size("cg")
    row_count, feat_width = embeddings.shape
    capacity = 2 * row_count // groups
    slot_count = groups * capacity
    member = lax.axis_index("cg") % TEAM
    unit_rows = normalize(embeddings)
    target = destination[:, 0]
    row_tag = jnp.where(valid_row == 1, 1, 0).astype(jnp.int32)
    places = jnp.arange(groups, dtype=jnp.int32)
    onehot = (target[:, None] == places[None, :]).astype(jnp.float32)
    row_order = jnp.arange(row_count, dtype=jnp.int32)
    earlier = (row_order[:, None] > row_order[None, :]).astype(jnp.float32)
    before = jnp.dot(earlier, onehot, precision=lax.Precision.HIGHEST)
    row_rank = jnp.sum(before * onehot, axis=1).astype(jnp.int32)
    row_slot = target * capacity + row_rank
    outgoing = jnp.zeros((slot_count, feat_width), jnp.bfloat16).at[row_slot].set(unit_rows)
    out_tags = jnp.zeros((slot_count,), jnp.int32).at[row_slot].set(row_tag)
    team_tags = jnp.repeat(out_tags.reshape(groups // TEAM, TEAM * capacity), TEAM, axis=0)
    positions = jnp.arange(slot_count, dtype=jnp.int32)
    own_key = member * slot_count + positions
    arrived, pool_tags = (
        lax.all_to_all(
            outgoing.reshape(groups, capacity, feat_width),
            "cg",
            split_axis=0,
            concat_axis=0,
            tiled=True,
        ),
        lax.all_to_all(team_tags, "cg", split_axis=0, concat_axis=0, tiled=True),
    )
    own_rows = arrived.reshape(slot_count, feat_width)

    def tags_of(owner_member):
        return lax.dynamic_slice_in_dim(pool_tags, owner_member * capacity, capacity, 1).reshape(
            slot_count
        )

    own_tag = tags_of(member)
    closest = closest_in(own_rows, own_tag, own_key, own_rows, own_tag, own_key)
    first_rows = from_partner(own_rows, "cg", 0)
    first_member = member ^ 1
    closest = jnp.maximum(
        closest,
        closest_in(
            own_rows,
            own_tag,
            own_key,
            first_rows,
            tags_of(first_member),
            first_member * slot_count + positions,
        ),
    )
    for held_rows, offset in ((own_rows, 2), (first_rows, 3)):
        far_rows = from_partner(held_rows, "cg", 1)
        owner_member = member ^ offset
        closest = jnp.maximum(
            closest,
            closest_in(
                own_rows,
                own_tag,
                own_key,
                far_rows,
                tags_of(owner_member),
                owner_member * slot_count + positions,
            ),
        )
    answers = lax.all_to_all(
        closest.reshape(groups, capacity), "cg", split_axis=0, concat_axis=0, tiled=True
    )
    return answers.reshape(slot_count)[row_slot]


MESH = pl.DeviceIdType.MESH
PLANES = 4
CHUNKS = 8
TAG_ROWS = 16
A, B, C, D = 4, 5, 6, 7


def pieces(row_count, feat_width):
    step = row_count // CHUNKS
    return [(row_count, TAG_ROWS, row_count)] + [(i * step, step, feat_width) for i in range(CHUNKS)]


def kernel(emb_ref, tag_ref, out_ref, held, cols, outbox, inbox, send_sem, recv_sem, back_send, back_recv):
    rows, width = emb_ref.shape
    parts = pieces(rows, width)
    group = lax.axis_index("groups")
    me = lax.axis_index("cg")
    other = 1 - group

    def turned(plane, of):
        return plane + of * (PLANES - 1 - 2 * plane)

    z, p = turned(me // TEAM, group), me % TEAM
    core_p = p + 1 - 2 * (p % 2)
    x_p = (p + 2) % TEAM
    diag_p = (core_p + 2) % TEAM

    def device(plane, place):
        return (group, turned(plane, group) * TEAM + place)

    def across(plane):
        return (other, turned(plane, other) * TEAM + p)

    barrier = pltpu.get_barrier_semaphore()
    for k in range(1, TEAM):
        pl.semaphore_signal(barrier, inc=1, device_id=device(z, (p + k) % TEAM), device_id_type=MESH)
    for k in range(1, PLANES):
        pl.semaphore_signal(barrier, inc=1, device_id=device((z + k) % PLANES, p), device_id_type=MESH)
    for k in range(1, PLANES):
        @pl.when((z == 2) | ((z > 0) & (k == 2)))
        def _():
            pl.semaphore_signal(barrier, inc=1, device_id=across(k), device_id_type=MESH)

    for i in range(4):
        block = pl.ds(i * (rows // 4), rows // 4)
        values = emb_ref[block, :].astype(jnp.float32)
        inv_scale = lax.rsqrt(jnp.mean(values * values, axis=1, keepdims=True) + epsilon)
        held[p, block, :] = (values * inv_scale * width ** (-0.5)).astype(jnp.bfloat16)
    held[p, pl.ds(rows, TAG_ROWS), pl.ds(0, rows)] = tag_ref[...]
    greeted = jnp.where(z == 2, PLANES - 1, jnp.where(z == 0, 0, 1))
    pl.semaphore_wait(barrier, TEAM - 1 + PLANES - 1 + greeted)

    def piece(slot, k):
        start, size, lanes = parts[k]
        return held.at[slot, pl.ds(start, size), pl.ds(0, lanes)]

    def copy(k, source, target, flow, to):
        return pltpu.make_async_remote_copy(
            src_ref=piece(source, k),
            dst_ref=piece(target, k),
            send_sem=send_sem.at[flow, k],
            recv_sem=recv_sem.at[target, k],
            device_id=to,
            device_id_type=MESH,
        )

    up, down = (z + 1) % PLANES, (z + PLANES - 1) % PLANES
    second = jnp.where(z == 1, B, A)
    core_own = lambda k: copy(k, p, p, 0, device(z, core_p))
    x_own = lambda k: copy(k, p, p, 1, device(z, x_p))
    core_pass = lambda k: copy(k, x_p, x_p, 2, device(z, core_p))
    up_own = lambda k: copy(k, p, A, 3, device(up, p))
    up_first = lambda k: copy(k, A, second, 4, device(up, p))
    up_second = lambda k: copy(k, B, B, 5, device(up, p))
    down_own = lambda k: copy(k, p, C, 6, device(down, p))
    out_relay = lambda k: copy(k, p, D, 7, across(2))
    relay_2 = lambda k: copy(k, D, A, 8, across(2))
    relay_3 = lambda k: copy(k, D, A, 9, across(3))
    every = range(len(parts))
    relayed = every[len(parts) - CHUNKS // 2:]

    def arrived(slot, k):
        copy(k, slot, slot, 0, device(z, core_p)).wait_recv()

    for k in every:
        pl.when((z == 0) if k in relayed else (z <= 1))(lambda: up_own(k).start())
        if k in relayed:
            pl.when(z == 1)(lambda: out_relay(k).start())
        pl.when(z == 3)(lambda: down_own(k).start())
        x_own(k).start()
    for k in every:
        core_own(k).start()

    def tag_lanes(slot):
        return held[slot, pl.ds(rows, TAG_ROWS), pl.ds(0, rows)].astype(jnp.float32)[0:1]

    def compare(slot, own, first, start=0, size=rows):
        tags = jnp.broadcast_to(tag_lanes(slot)[:, start:start + size], (128, size)).T
        tags = jnp.concatenate([tags] * (rows // 128), axis=1)

        def step(q, best):
            similar = lax.dot_general(
                held[slot, pl.ds(start, size), :],
                held[q, pl.ds(0, rows), :],
                (((1,), (1,)), ((), ())),
                preferred_element_type=jnp.float32,
            )
            other = tag_lanes(q)
            match = tags == jnp.where(other < 0, -2.0, other)
            if own:
                here = lax.broadcasted_iota(jnp.int32, (size, rows), 0)
                there = lax.broadcasted_iota(jnp.int32, (size, rows), 1)
                match = match & (here + jnp.where(q == p, 0, rows) != there)
            similar = jnp.where(match, similar, -1.0)
            if not own:
                top = jnp.broadcast_to(jnp.max(similar, axis=0, keepdims=True), (8, rows))
                cols[q] = top if first else jnp.maximum(cols[q], top)
            for i in range(rows // 128):
                best = jnp.maximum(best, similar[:, i * 128:(i + 1) * 128])
            return best

        best = lax.fori_loop(0, TEAM, step, jnp.full((size, 128), -1.0, jnp.float32))
        return jnp.broadcast_to(jnp.max(best.T, axis=0, keepdims=True), (8, size))

    def back(n, target, to):
        return pltpu.make_async_remote_copy(
            src_ref=outbox.at[n, pl.ds(0, 1)],
            dst_ref=inbox.at[target, pl.ds(0, 1)],
            send_sem=back_send.at[n],
            recv_sem=back_recv.at[target],
            device_id=to,
            device_id_type=MESH,
        )

    back_a = lambda: back(0, z, device(jnp.where(z == 1, 0, 1), p))
    back_b = lambda: back(1, z, device(0, p))
    back_c = lambda: back(2, z, device(3, p))
    back_q = lambda k: back(2 + k, PLANES + p, device(z, (p + k) % TEAM))

    def returned(target):
        back(0, target, device(z, core_p)).wait_recv()

    def pump(k):
        @pl.when(z >= 2)
        def _():
            arrived(B, k)
            pl.when(z == 2)(lambda: up_second(k).start())

    for k in every:
        if k + len(relayed) in relayed:
            @pl.when(z == 2)
            def _():
                arrived(D, k + len(relayed))
                relay_2(k + len(relayed)).start()
                relay_3(k + len(relayed)).start()

        if k in relayed:
            pump(k - relayed[0])

        @pl.when(z >= 1)
        def _():
            arrived(A, k)
            pl.when((z == 1) if k in relayed else (z <= 2))(lambda: up_first(k).start())

    for k in every:
        arrived(x_p, k)
        core_pass(k).start()
    for k in every:
        arrived(core_p, k)
    for k in every:
        arrived(diag_p, k)

    @pl.when(z >= 1)
    def _():
        outbox[0] = compare(A, False, True)
        back_a().start()

    out_ref[...] = compare(p, True, False)
    pump(4)

    @pl.when(z == 2)
    def _():
        for k in every:
            arrived(C, k)
        outbox[2] = compare(C, False, False)
        back_c().start()

    half = rows // 2

    @pl.when(z >= 2)
    def _():
        outbox[1, :, pl.ds(0, half)] = compare(B, False, False, 0, half)

    for k in every[5:]:
        pump(k)

    @pl.when(z >= 2)
    def _():
        outbox[1, :, pl.ds(half, half)] = compare(B, False, False, half, half)
        back_b().start()

    @pl.when(z >= 1)
    def _():
        for k in range(1, TEAM):
            outbox[2 + k] = cols[(p + k) % TEAM]
            back_q(k).start()

    @pl.when(z >= 1)
    def _():
        best = cols[p]
        for k in range(1, TEAM):
            returned(PLANES + (p + k) % TEAM)
            best = jnp.maximum(best, inbox[PLANES + (p + k) % TEAM, pl.ds(0, 1)])
        out_ref[...] = jnp.maximum(out_ref[...], best)

    for source, readers in ((1, z == 0), (2, (z == 0) | (z == 1) | (z == 3)), (3, z <= 1)):
        @pl.when(readers)
        def _():
            returned(source)
            out_ref[...] = jnp.maximum(out_ref[...], inbox[source, pl.ds(0, 1)])

    for k in every:
        core_own(k).wait_send()
        x_own(k).wait_send()
        core_pass(k).wait_send()
        pl.when((z == 0) if k in relayed else (z <= 1))(lambda: up_own(k).wait_send())
        pl.when((z == 1) if k in relayed else ((z == 1) | (z == 2)))(lambda: up_first(k).wait_send())
        if k in relayed:
            pl.when(z == 1)(lambda: out_relay(k).wait_send())
            pl.when(z == 2)(lambda: relay_2(k).wait_send())
            pl.when(z == 2)(lambda: relay_3(k).wait_send())
        pl.when(z == 2)(lambda: up_second(k).wait_send())
        pl.when(z == 3)(lambda: down_own(k).wait_send())

    @pl.when(z >= 1)
    def _():
        back_a().wait_send()
        for k in range(1, TEAM):
            back_q(k).wait_send()

    pl.when(z >= 2)(lambda: back_b().wait_send())
    pl.when(z == 2)(lambda: back_c().wait_send())


def in_planes(embeddings, destination, valid_row):
    rows, width = embeddings.shape
    tag = jnp.where(valid_row == 1, destination[:, 0] // TEAM, -1).astype(jnp.bfloat16)
    count = len(pieces(rows, width))
    vmem = pl.BlockSpec(memory_space=pltpu.VMEM)
    closest = pl.pallas_call(
        kernel,
        out_shape=jax.ShapeDtypeStruct((8, rows), jnp.float32),
        in_specs=[vmem, vmem],
        out_specs=vmem,
        scratch_shapes=[
            pltpu.VMEM((TEAM + 4, rows + TAG_ROWS, width), jnp.bfloat16),
            pltpu.VMEM((TEAM, 8, rows), jnp.float32),
            pltpu.VMEM((6, 8, rows), jnp.float32),
            pltpu.VMEM((PLANES + TEAM, 8, rows), jnp.float32),
            pltpu.SemaphoreType.DMA((10, count)),
            pltpu.SemaphoreType.DMA((TEAM + 4, count)),
            pltpu.SemaphoreType.DMA((6,)),
            pltpu.SemaphoreType.DMA((PLANES + TEAM,)),
        ],
        compiler_params=pltpu.CompilerParams(
            collective_id=0, has_side_effects=True, vmem_limit_bytes=32 * 1024 * 1024
        ),
    )(embeddings, jnp.broadcast_to(tag[None, :], (TAG_ROWS, rows)))
    return closest[0]


def solution(mesh):
    return jax.shard_map(
        in_planes if dict(mesh.shape) == {"groups": 2, "cg": PLANES * TEAM} else on_device,
        mesh=mesh,
        in_specs=(P(("groups", "cg"), None), P(("groups", "cg"), None), P(("groups", "cg"))),
        out_specs=P(("groups", "cg")),
        check_vma=False,
    )
```
